32 devices in a mesh: seq: 16 (over z, y, core), row: 2 (over x).
Axes of the slice: x: 2, y: 2, z: 4, core: 2. Of those that a mesh axis runs over, the one named last changes fastest.
Arguments:
- inputs: bfloat16 [2, 32768, 768], P('row', 'seq'), may hold values from -6 to 6
- w_query: bfloat16 [768, 768], replicated, may hold values from -0.21875 to 0.21875
- w_key: bfloat16 [768, 768], replicated, may hold values from -0.21875 to 0.21875
- w_value: bfloat16 [768, 768], replicated, may hold values from -0.21875 to 0.21875
- w_out: bfloat16 [768, 768], replicated, may hold values from -3 to 3
- w_up: bfloat16 [768, 3072], replicated, may hold values from -0.21875 to 0.21875
- w_down: bfloat16 [3072, 768], replicated, may hold values from -0.109375 to 0.109375
- b_query: bfloat16 [768], replicated, may hold values from -3 to 3
- b_key: bfloat16 [768], replicated, may hold values from -3 to 3
- b_value: bfloat16 [768], replicated, may hold values from -3 to 3
- b_out: bfloat16 [768], replicated, may hold values from -3 to 3
- b_up: bfloat16 [3072], replicated, may hold values from -3 to 3
- b_down: bfloat16 [768], replicated, may hold values from -3 to 3
- norm1_gain: bfloat16 [768], replicated, may hold values from 0.5 to 1.5
- norm1_shift: bfloat16 [768], replicated, may hold values from -3 to 3
- norm2_gain: bfloat16 [768], replicated, may hold values from 0.5 to 1.5
- norm2_shift: bfloat16 [768], replicated, may hold values from -3 to 3
- head_feature_directions: bfloat16 [12, 256, 64], replicated, may hold values from -4 to 4
- seq_lengths: int32 [2, 6], P('row'), may hold values from 1024 to 20480, as said below
- seq_starts: int32 [2, 6], P('row'), may hold values from 0 to 30720, as said below
- cotangent: bfloat16 [2, 32768, 768], P('row', 'seq'), may hold values from -6 to 6
Outputs:
- layer_out: float32 [2, 32768, 768], P('row', 'seq')
- input_grad: float32 [2, 32768, 768], P('row', 'seq')
- grad_w_query: float32 [768, 768], replicated
- grad_w_key: float32 [768, 768], replicated
- grad_w_value: float32 [768, 768], replicated
- grad_w_out: float32 [768, 768], replicated
- grad_w_up: float32 [768, 3072], replicated
- grad_w_down: float32 [3072, 768], replicated
- grad_b_query: float32 [768], replicated
- grad_b_key: float32 [768], replicated
- grad_b_value: float32 [768], replicated
- grad_b_out: float32 [768], replicated
- grad_b_up: float32 [3072], replicated
- grad_b_down: float32 [768], replicated
- grad_norm1_gain: float32 [768], replicated
- grad_norm1_shift: float32 [768], replicated
- grad_norm2_gain: float32 [768], replicated
- grad_norm2_shift: float32 [768], replicated
The draws below stay inside these ranges and needn't reach their ends.
Inputs may be any that keep to these rules, and one draw needn't show every extreme that they name: Each row is split into six buckets laid end to end in an order that differs from row to row. The first bucket holds 20480 token places, the second holds 4096, and each of the last four holds 2048; seq_starts gives each bucket's first place in its row. The sequence of a bucket occupies the first seq_lengths places of that bucket; the rest is padding. The first bucket is always full; every other bucket holds at least its capacity minus 2048 // 2 tokens.
All inputs are finite; a program needn't handle non-finite values.
Results may differ from the reference program's by a relative error of at most 0.04.
Values sent between devices are 32-bit elements; how exact they have to be, the bound alone decides.
No kernel may reach another device: no remote copies, remote signals or barrier semaphores. Data moves between devices by JAX's collectives and lax.ppermute only.
A program may use at most 384 MiB of HBM per device.

```python
import math
import jax
import jax.numpy as jnp
from jax import lax

D = 768
H = 12
HEAD_SIZE = 64
FF = 3072
M = 256
TOK_DEV = 2048
ROWS = 2
ROW_TOKENS = 32768
WIDEST_LIMIT = 20480
MEDIAN_LIMIT = 4096
NARROW_LIMIT = 2048


def draw_seq_starts(key, part):
    key = jax.random.fold_in(key, 3)
    group_limits = jnp.array([WIDEST_LIMIT, MEDIAN_LIMIT, NARROW_LIMIT, NARROW_LIMIT, NARROW_LIMIT, NARROW_LIMIT], jnp.int32)
    order_key, last_key = jax.random.split(key)
    row_keys = jax.random.split(order_key, ROWS)
    ranking_permutations = jax.vmap(lambda row_key: jax.random.permutation(row_key, 6))(row_keys).astype(jnp.int32)
    chosen = jax.random.randint(last_key, (), 2, 6).astype(jnp.int32)
    first_row = ranking_permutations[0]
    places = jnp.arange(6, dtype=jnp.int32)
    fixed_row = jnp.where(first_row == chosen, first_row[5], jnp.where(places == 5, chosen, first_row)).astype(jnp.int32)
    ranking_permutations = ranking_permutations.at[0].set(fixed_row)
    assigned_items = jnp.take(group_limits, ranking_permutations)
    openings = jnp.cumsum(assigned_items, axis=1) - assigned_items
    matches = (ranking_permutations[:, :, None] == jnp.arange(6, dtype=jnp.int32)[None, None, :]).astype(jnp.int32)
    return jnp.sum(matches * openings[:, :, None], axis=1).astype(jnp.int32)


def draw_seq_lengths(key, part):
    key = jax.random.fold_in(key, 7)
    group_limits = jnp.array([WIDEST_LIMIT, MEDIAN_LIMIT, NARROW_LIMIT, NARROW_LIMIT, NARROW_LIMIT, NARROW_LIMIT], jnp.int32)
    absent_items = jax.random.randint(key, (ROWS, 6), 0, TOK_DEV // 2 + 1).astype(jnp.int32)
    absent_items = absent_items * (jnp.arange(6, dtype=jnp.int32) > 0).astype(jnp.int32)[None, :]
    return (group_limits[None, :] - absent_items).astype(jnp.int32)


def levels(stream_key, dims, shards, low, largest):
    def one(dim, blocks):
        draws = jax.random.uniform(jax.random.fold_in(jax.random.fold_in(stream_key, 6), dim), (blocks,), jnp.float32, low / len(shards), largest / len(shards))
        return jnp.repeat(jnp.exp(draws), dims[dim] // blocks).reshape((-1,) + (1,) * (len(dims) - dim - 1))

    loudness = one(*shards[0])
    for cut in shards[1:]:
        loudness = loudness * one(*cut)
    return loudness


def centred(own_key, dims, deviation, limit, cuts=(), kind=jnp.bfloat16):
    entries = deviation * jax.random.normal(own_key, dims, jnp.float32)
    if cuts:
        entries = entries * levels(own_key, dims, cuts, -0.22, 0.18)
    return jnp.clip(entries, -limit, limit).astype(kind)


def setup_inputs(seed: int = 0) -> dict:
    splits = jax.random.split(jax.random.key(seed), 22)
    return {
        "inputs": centred(splits[0], (ROWS, ROW_TOKENS, D), 1.0, 6.0, ((0, 2), (1, 16))),
        "w_query": centred(splits[1], (D, D), D ** -0.5, 0.21875),
        "w_key": centred(splits[2], (D, D), D ** -0.5, 0.21875),
        "w_value": centred(splits[3], (D, D), D ** -0.5, 0.21875),
        "w_out": centred(splits[4], (D, D), 4 ** -0.5, 3.0),
        "w_up": centred(splits[5], (D, FF), D ** -0.5, 0.21875),
        "w_down": centred(splits[6], (FF, D), FF ** -0.5, 0.109375),
        "b_query": centred(splits[7], (D,), 0.5, 3.0),
        "b_key": centred(splits[8], (D,), 0.5, 3.0),
        "b_value": centred(splits[9], (D,), 0.5, 3.0),
        "b_out": centred(splits[10], (D,), 0.5, 3.0),
        "b_up": centred(splits[11], (FF,), 0.5, 3.0),
        "b_down": centred(splits[12], (D,), 0.5, 3.0),
        "norm1_gain": jnp.clip(1.0 + 0.1 * jax.random.normal(splits[13], (D,), jnp.float32), 0.5, 1.5).astype(jnp.bfloat16),
        "norm1_shift": centred(splits[14], (D,), 0.5, 3.0),
        "norm2_gain": jnp.clip(1.0 + 0.1 * jax.random.normal(splits[15], (D,), jnp.float32), 0.5, 1.5).astype(jnp.bfloat16),
        "norm2_shift": centred(splits[16], (D,), 0.5, 3.0),
        "head_feature_directions": centred(splits[17], (H, M, HEAD_SIZE), 1.0, 4.0),
        "seq_lengths": draw_seq_lengths(jax.random.fold_in(splits[21], 71), 0),
        "seq_starts": draw_seq_starts(jax.random.fold_in(splits[21], 71), 0),
        "cotangent": centred(splits[20], (ROWS, ROW_TOKENS, D), 1.0, 6.0, ((0, 2), (1, 16))),
    }


@jax.custom_vjp
def low(v):
    return lax.optimization_barrier(v.astype(jnp.bfloat16)).astype(jnp.float32)

@jax.custom_vjp
def low_back(v):
    return v

def low_keep(v):
    return (low(v), None)

def low_pass(kept, grad):
    return (grad,)

def back_keep(v):
    return (v, None)

def back_low(kept, grad):
    return (low(grad),)
low.defvjp(low_keep, low_pass)
low_back.defvjp(back_keep, back_low)
EPSILON = 1e-05
TOP_PRECISION = lax.Precision.HIGHEST

def product(left, right):
    return jnp.dot(left, right, precision=TOP_PRECISION, preferred_element_type=jnp.float32)

def norm_layer(hidden, gain_vec, offset_vec):
    centre = hidden - lax.optimization_barrier(jnp.mean(hidden, axis=-1, keepdims=True))
    spread = lax.optimization_barrier(jnp.mean(centre * centre, axis=-1, keepdims=True))
    return centre * lax.rsqrt(spread + EPSILON) * gain_vec + offset_vec

def positive_features(raw_logits, rounded_values):
    square = lax.optimization_barrier(jnp.sum(rounded_values * rounded_values, axis=-1, keepdims=True))
    return jnp.exp(raw_logits - square * (0.5 / math.sqrt(HEAD_SIZE))) * (1.0 / math.sqrt(M))

def feature_map(rounded_values, head_feature_directions):
    raw_logits = low_back(HEAD_SIZE ** (-0.25) * jnp.einsum('qnub,uob->qnuo', rounded_values, head_feature_directions, precision=TOP_PRECISION))
    return low(positive_features(raw_logits, rounded_values))

def layer(inputs, w_query, w_key, w_value, w_out, w_up, w_down, b_query, b_key, b_value, b_out, b_up, b_down, norm1_gain, norm1_shift, norm2_gain, norm2_shift, head_feature_directions, seq_lengths, seq_starts):
    tokens = inputs.reshape(ROWS * ROW_TOKENS, D)
    queries = low(low_back(product(tokens, w_query) + b_query)).reshape(ROWS, ROW_TOKENS, H, HEAD_SIZE)
    keys_all = low(low_back(product(tokens, w_key) + b_key)).reshape(ROWS, ROW_TOKENS, H, HEAD_SIZE)
    values_all = low(low_back(product(tokens, w_value) + b_value)).reshape(ROWS, ROW_TOKENS, H, HEAD_SIZE)
    query_feat = feature_map(queries, head_feature_directions)
    key_features = feature_map(keys_all, head_feature_directions)
    group_limits = [WIDEST_LIMIT, MEDIAN_LIMIT] + [NARROW_LIMIT] * 4
    outputs = []
    for row_index in range(ROWS):
        attended = jnp.zeros((ROW_TOKENS, H, HEAD_SIZE), jnp.float32)
        for group_number, group_limit in enumerate(group_limits):
            opening = seq_starts[row_index, group_number].astype(jnp.int32)
            query_matrix = lax.dynamic_slice_in_dim(query_feat[row_index], opening, group_limit, 0)
            key_matrix = lax.dynamic_slice_in_dim(key_features[row_index], opening, group_limit, 0)
            value_matrix = lax.dynamic_slice_in_dim(values_all[row_index], opening, group_limit, 0)
            present = (jnp.arange(group_limit, dtype=jnp.int32) < seq_lengths[row_index, group_number].astype(jnp.int32)).astype(jnp.float32)
            key_matrix = key_matrix * present[:, None, None]
            key_value_summary = low(low_back(jnp.einsum('uzl,uzy->zly', key_matrix, value_matrix, precision=TOP_PRECISION)))
            normaliser = lax.optimization_barrier(jnp.sum(key_matrix, axis=0))
            attention_numerator = low_back(jnp.einsum('pez,ezi->pei', query_matrix, key_value_summary, precision=TOP_PRECISION))
            denominator = jnp.einsum('thm,hm->th', query_matrix, normaliser, precision=TOP_PRECISION)
            attended = lax.dynamic_update_slice_in_dim(attended, attention_numerator / denominator[:, :, None], opening, 0)
        outputs.append(attended)
    mixture = low(jnp.stack(outputs).reshape(ROWS * ROW_TOKENS, D))
    branch = low_back(product(mixture, w_out) + b_out)
    normed1 = norm_layer(tokens + branch, norm1_gain, norm1_shift)
    pre_act = low_back(product(low(normed1), w_up) + b_up)
    activation = low(jax.nn.gelu(pre_act))
    feed_out = low_back(product(activation, w_down) + b_down)
    result = norm_layer(normed1 + feed_out, norm2_gain, norm2_shift)
    return result.reshape(ROWS, ROW_TOKENS, D)

def reference(inputs, w_query, w_key, w_value, w_out, w_up, w_down, b_query, b_key, b_value, b_out, b_up, b_down, norm1_gain, norm1_shift, norm2_gain, norm2_shift, head_feature_directions, seq_lengths, seq_starts, cotangent):
    params = [inputs, w_query, w_key, w_value, w_out, w_up, w_down, b_query, b_key, b_value, b_out, b_up, b_down, norm1_gain, norm1_shift, norm2_gain, norm2_shift]
    params = [entry.astype(jnp.float32) for entry in params]
    maps_wide = head_feature_directions.astype(jnp.float32)

    def forward(*input_values):
        return layer(*input_values, maps_wide, seq_lengths, seq_starts)
    result, pullback = jax.vjp(forward, *params)
    grads = pullback(cotangent.astype(jnp.float32))
    return (result.astype(jnp.float32), grads[0], grads[1], grads[2], grads[3], grads[4], grads[5], grads[6], grads[7], grads[8], grads[9], grads[10], grads[11], grads[12], grads[13], grads[14], grads[15], grads[16])
```

```python
import math

import jax
import jax.numpy as jnp
from jax import lax
from jax.sharding import PartitionSpec as P

EPSILON = 1e-05


def norm_layer(hidden, gain_vec, offset_vec):
    centre = hidden - jnp.mean(hidden, axis=-1, keepdims=True)
    spread = jnp.mean(centre * centre, axis=-1, keepdims=True)
    return centre * lax.rsqrt(spread + EPSILON) * gain_vec + offset_vec


def positive_features(raw_logits, rounded_values, norm_weight, prefactor):
    widened = rounded_values.astype(jnp.float32)
    square = jnp.sum(widened * widened, axis=-1, keepdims=True)
    return jnp.exp(raw_logits - square * norm_weight) * prefactor


def feature_logits(rounded_values, head_feature_directions, feature_scale):
    return feature_scale * jnp.einsum(
        "nlr,lur->nlu", rounded_values, head_feature_directions, preferred_element_type=jnp.float32
    )


def feature_back(
    feat_grad, feat_value, rounded_values, head_feature_directions, feature_scale, norm_weight
):
    logit_grad = feat_grad * feat_value
    through = feature_scale * jnp.einsum(
        "pez,ezi->pei",
        logit_grad.astype(jnp.bfloat16),
        head_feature_directions,
        preferred_element_type=jnp.float32,
    )
    return through - 2.0 * norm_weight * jnp.sum(
        logit_grad, axis=-1, keepdims=True
    ) * rounded_values.astype(jnp.float32)


def bits_of(axis):
    return [(axis, bit) for bit in range(lax.axis_size(axis).bit_length() - 1)]


def coordinate(tag):
    return (lax.axis_index(tag[0]) >> tag[1]) & 1


def exchange(sent, tag):
    pairs = [(i, i ^ (1 << tag[1])) for i in range(lax.axis_size(tag[0]))]
    return lax.ppermute(sent, tag[0], pairs)


def halve_sum(array, tags, order):
    left = list(tags)
    for tag in order:
        where = left.index(tag)
        mine = coordinate(tag)
        sent = lax.dynamic_index_in_dim(array, 1 - mine, where, keepdims=False)
        kept = lax.dynamic_index_in_dim(array, mine, where, keepdims=False)
        array = kept + exchange(sent, tag)
        left.pop(where)
    return array


def double_gather(block, order):
    for tag in reversed(order):
        other = exchange(block, tag)
        mine = coordinate(tag) == 0
        block = jnp.stack([jnp.where(mine, block, other), jnp.where(mine, other, block)])
    return block


def weight_tags():
    seq, row = bits_of("seq"), bits_of("row")
    first = seq[:1] + row + seq[1:]
    second = seq[:2] + row + seq[2:]
    return first, second


def scatter_chunks(chunks):
    first, second = weight_tags()
    out = []
    for number, chunk in enumerate(chunks):
        order = second if number % 2 else first
        rows = chunk.shape[0] >> len(first)
        out.append(halve_sum(chunk.reshape((2,) * len(first) + (rows, chunk.shape[1])), first, order))
    return out


def gather_blocks(block):
    whole = lax.all_gather(block, ("seq", "row"), axis=0, tiled=False)
    seq, row = bits_of("seq"), bits_of("row")
    tags = seq[::-1] + row[::-1]
    first, _ = weight_tags()
    whole = whole.reshape((2,) * len(tags) + block.shape)
    places = [tags.index(tag) for tag in first]
    rest = list(range(len(tags), len(tags) + block.ndim))
    return whole.transpose(places + rest).reshape((1 << len(tags),) + block.shape)


def sum_devices(array):
    for tag in weight_tags()[0]:
        array = array + exchange(array, tag)
    return array


def bucket_sum(onehot, shared, summary_part, normaliser_part):
    heads, features, width = summary_part.shape
    tags = bits_of("seq")
    unit = 8 << len(tags)
    rows = heads * width + heads
    padded = -(-rows // unit) * unit
    part = jnp.concatenate(
        [
            summary_part.transpose(0, 2, 1).reshape(heads * width, features),
            normaliser_part,
            jnp.zeros((padded - rows, features), jnp.float32),
        ]
    )
    slots = onehot[:shared].reshape(1, shared, 1, 1)
    blocks = part.reshape(1 << len(tags), 1, padded >> len(tags), features) * slots
    blocks = blocks.reshape((2,) * len(tags) + blocks.shape[1:])
    order = tags
    summed = double_gather(halve_sum(blocks, tags, order), order)
    summed = jnp.sum(summed.reshape((1 << len(tags),) + summed.shape[len(tags):]) * slots, axis=1)
    alone = 1.0 - jnp.sum(onehot[:shared])
    summed = summed.reshape(padded, features) + alone * part
    summary = summed[: heads * width].reshape(heads, width, features).transpose(0, 2, 1)
    return summary, summed[heads * width : rows]


def on_device(
    inputs,
    w_query,
    w_key,
    w_value,
    w_out,
    w_up,
    w_down,
    b_query,
    b_key,
    b_value,
    b_out,
    b_up,
    b_down,
    norm1_gain,
    norm1_shift,
    norm2_gain,
    norm2_shift,
    head_feature_directions,
    seq_lengths,
    seq_starts,
    cotangent,
):
    tokens = inputs.shape[1]
    model_width = inputs.shape[2]
    head_count, feature_rows, head_dim = head_feature_directions.shape
    feature_scale = head_dim ** (-0.25)
    norm_weight = 0.5 / math.sqrt(head_dim)
    prefactor = 1.0 / math.sqrt(feature_rows)
    blocks = lax.axis_size("seq")
    position = lax.axis_index("seq")
    widths = [5 * blocks // 8, blocks // 8] + [blocks // 16] * 4
    shared = sum(width > 1 for width in widths)
    group_limit = jnp.array(widths, jnp.int32) * tokens
    openings = seq_starts[0]
    lengths_row = seq_lengths[0]
    block_start = position * tokens
    member = (openings <= block_start) & (block_start < openings + group_limit)
    placement = block_start + jnp.arange(tokens, dtype=jnp.int32)[:, None] - openings[None, :]
    live_token_mask = jnp.sum(
        jnp.where(member[None, :] & (placement < lengths_row[None, :]), 1.0, 0.0), axis=1
    ).astype(jnp.float32)
    onehot = member.astype(jnp.float32)
    tokens_in = inputs[0]

    def project(weight, bias):
        return jnp.dot(tokens_in, weight, preferred_element_type=jnp.float32) + bias.astype(
            jnp.float32
        )

    queries = project(w_query, b_query).astype(jnp.bfloat16).reshape(tokens, head_count, head_dim)
    keys_in = project(w_key, b_key).astype(jnp.bfloat16).reshape(tokens, head_count, head_dim)
    input_values = (
        project(w_value, b_value).astype(jnp.bfloat16).reshape(tokens, head_count, head_dim)
    )
    query_feat = positive_features(
        feature_logits(queries, head_feature_directions, feature_scale),
        queries,
        norm_weight,
        prefactor,
    )
    key_features = positive_features(
        feature_logits(keys_in, head_feature_directions, feature_scale),
        keys_in,
        norm_weight,
        prefactor,
    )
    query_reduced = query_feat.astype(jnp.bfloat16)
    query_wide = query_reduced.astype(jnp.float32)
    key_reduced = (
        key_features.astype(jnp.bfloat16) * live_token_mask.astype(jnp.bfloat16)[:, None, None]
    )
    summary_part = jnp.einsum(
        "uzl,uzy->zly", key_reduced, input_values, preferred_element_type=jnp.float32
    )
    normaliser_part = jnp.sum(key_reduced.astype(jnp.float32), axis=0)
    key_value_summary, normaliser = bucket_sum(onehot, shared, summary_part, normaliser_part)
    summary_reduced = key_value_summary.astype(jnp.bfloat16)
    attention_numerator = jnp.einsum(
        "pez,ezi->pei", query_reduced, summary_reduced, preferred_element_type=jnp.float32
    )
    denominator = jnp.einsum("thm,hm->th", query_wide, normaliser, precision=lax.Precision.HIGHEST)
    mixture = (
        (attention_numerator / denominator[:, :, None])
        .astype(jnp.bfloat16)
        .reshape(tokens, model_width)
    )
    branch = jnp.dot(mixture, w_out, preferred_element_type=jnp.float32) + b_out.astype(jnp.float32)
    residual = tokens_in.astype(jnp.float32) + branch
    normed1, first_pull = jax.vjp(
        norm_layer, residual, norm1_gain.astype(jnp.float32), norm1_shift.astype(jnp.float32)
    )
    normed_low = normed1.astype(jnp.bfloat16)
    pre_act = jnp.dot(normed_low, w_up, preferred_element_type=jnp.float32) + b_up.astype(
        jnp.float32
    )
    activation, gelu_pull = jax.vjp(jax.nn.gelu, pre_act)
    activation_low = activation.astype(jnp.bfloat16)
    feed_out = jnp.dot(activation_low, w_down, preferred_element_type=jnp.float32) + b_down.astype(
        jnp.float32
    )
    result, second_pull = jax.vjp(
        norm_layer,
        normed1 + feed_out,
        norm2_gain.astype(jnp.float32),
        norm2_shift.astype(jnp.float32),
    )
    seed_grad = cotangent[0].astype(jnp.float32)
    second_grad, gain2_grad, shift2_grad = second_pull(seed_grad)
    feed_grad = second_grad.astype(jnp.bfloat16)
    grad_down = jnp.einsum(
        "tf,td->fd", activation_low, feed_grad, preferred_element_type=jnp.float32
    )
    grad_bdown = jnp.sum(feed_grad.astype(jnp.float32), axis=0)
    active_grad = jnp.einsum("td,fd->tf", feed_grad, w_down, preferred_element_type=jnp.float32)
    pre_grad = gelu_pull(active_grad)[0].astype(jnp.bfloat16)
    grad_up = jnp.einsum("td,tf->df", normed_low, pre_grad, preferred_element_type=jnp.float32)
    grad_bup = jnp.sum(pre_grad.astype(jnp.float32), axis=0)
    normed_grad = second_grad + jnp.einsum(
        "tf,df->td", pre_grad, w_up, preferred_element_type=jnp.float32
    )
    residual_grad, gain1_grad, shift1_grad = first_pull(normed_grad)
    branch_grad = residual_grad.astype(jnp.bfloat16)
    grad_out = jnp.einsum("tk,td->kd", mixture, branch_grad, preferred_element_type=jnp.float32)
    grad_bout = jnp.sum(branch_grad.astype(jnp.float32), axis=0)
    attended_grad = jnp.einsum(
        "td,kd->tk", branch_grad, w_out, preferred_element_type=jnp.float32
    ).reshape(tokens, head_count, head_dim)
    numerator_gradient = (attended_grad / denominator[:, :, None]).astype(jnp.bfloat16)
    denominator_grad = -jnp.sum(attended_grad * attention_numerator, axis=-1) / (
        denominator * denominator
    )
    qfeat_grad = (
        jnp.einsum(
            "nlr,lur->nlu", numerator_gradient, summary_reduced, preferred_element_type=jnp.float32
        )
        + denominator_grad[:, :, None] * normaliser[None]
    )
    summary_grad_part = jnp.einsum(
        "uzl,uzy->zly", query_reduced, numerator_gradient, preferred_element_type=jnp.float32
    )
    normaliser_grad_part = jnp.einsum(
        "thm,th->hm", query_wide, denominator_grad, precision=lax.Precision.HIGHEST
    )
    summary_grad, normaliser_grad = bucket_sum(
        onehot, shared, summary_grad_part, normaliser_grad_part
    )
    summary_gradient_reduced = summary_grad.astype(jnp.bfloat16)
    kfeat_grad = (
        jnp.einsum(
            "nlr,lur->nlu",
            input_values,
            summary_gradient_reduced,
            preferred_element_type=jnp.float32,
        )
        + normaliser_grad[None]
    ) * live_token_mask[:, None, None]
    value_grad = (
        jnp.einsum(
            "pez,ezi->pei",
            key_reduced,
            summary_gradient_reduced,
            preferred_element_type=jnp.float32,
        )
        .astype(jnp.bfloat16)
        .reshape(tokens, model_width)
    )
    query_grad = (
        feature_back(
            qfeat_grad, query_feat, queries, head_feature_directions, feature_scale, norm_weight
        )
        .astype(jnp.bfloat16)
        .reshape(tokens, model_width)
    )
    key_grad = (
        feature_back(
            kfeat_grad, key_features, keys_in, head_feature_directions, feature_scale, norm_weight
        )
        .astype(jnp.bfloat16)
        .reshape(tokens, model_width)
    )

    def weight_grad(token_grad):
        return jnp.einsum("td,tk->dk", tokens_in, token_grad, preferred_element_type=jnp.float32)

    def back_through(token_grad, weight):
        return jnp.einsum("tk,dk->td", token_grad, weight, preferred_element_type=jnp.float32)

    input_grad = (
        residual_grad
        + back_through(query_grad, w_query)
        + back_through(key_grad, w_key)
        + back_through(value_grad, w_value)
    )
    ff = grad_up.shape[1]

    def columns(matrix):
        half = matrix.shape[1] // 2
        return [matrix[:, :half], matrix[:, half:]]

    down_blocks = scatter_chunks(columns(grad_down))
    up_blocks = scatter_chunks(columns(grad_up))
    first_blocks = scatter_chunks([grad_out, weight_grad(query_grad)])
    last_blocks = scatter_chunks([weight_grad(key_grad), weight_grad(value_grad)])
    whole_down = gather_blocks(jnp.concatenate(down_blocks, axis=1)).reshape(ff, model_width)
    whole_up = gather_blocks(jnp.concatenate(up_blocks, axis=1)).reshape(model_width, ff)
    whole_first = gather_blocks(jnp.stack(first_blocks))
    whole_last = gather_blocks(jnp.stack(last_blocks))

    def square(whole, which):
        return whole[:, which].reshape(model_width, model_width)

    small = [
        jnp.sum(query_grad.astype(jnp.float32), axis=0),
        jnp.sum(key_grad.astype(jnp.float32), axis=0),
        jnp.sum(value_grad.astype(jnp.float32), axis=0),
        grad_bout,
        grad_bup,
        grad_bdown,
        gain1_grad,
        shift1_grad,
        gain2_grad,
        shift2_grad,
    ]
    small_sum = sum_devices(jnp.concatenate(small).reshape(-1, model_width)).reshape(-1)
    pieces = [
        square(whole_first, 1),
        square(whole_last, 0),
        square(whole_last, 1),
        square(whole_first, 0),
        whole_up,
        whole_down,
    ]
    cursor = 0
    for gradient in small:
        pieces.append(small_sum[cursor : cursor + gradient.size])
        cursor = cursor + gradient.size
    return (
        result[None],
        input_grad[None],
        pieces[0],
        pieces[1],
        pieces[2],
        pieces[3],
        pieces[4],
        pieces[5],
        pieces[6],
        pieces[7],
        pieces[8],
        pieces[9],
        pieces[10],
        pieces[11],
        pieces[12],
        pieces[13],
        pieces[14],
        pieces[15],
    )


def solution(mesh):
    return jax.shard_map(
        on_device,
        mesh=mesh,
        in_specs=(
            P("row", "seq", None),
            P(),
            P(),
            P(),
            P(),
            P(),
            P(),
            P(),
            P(),
            P(),
            P(),
            P(),
            P(),
            P(),
            P(),
            P(),
            P(),
            P(),
            P("row", None),
            P("row", None),
            P("row", "seq", None),
        ),
        out_specs=(
            P("row", "seq", None),
            P("row", "seq", None),
            P(),
            P(),
            P(),
            P(),
            P(),
            P(),
            P(),
            P(),
            P(),
            P(),
            P(),
            P(),
            P(),
            P(),
            P(),
            P(),
        ),
        check_vma=False,
    )
```

```python
import functools
import math
import typing

import jax
import jax.numpy as jnp
from jax import lax
from jax.experimental import pallas as pl
from jax.experimental.pallas import tpu as pltpu
from jax.sharding import PartitionSpec as P

EPSILON = 1e-05
F32, BF16 = jnp.float32, jnp.bfloat16
MIB = 1 << 20
GELU_SCALE = math.sqrt(2.0 / math.pi)
GELU_CUBE = 0.044715


class Consts(typing.NamedTuple):
    scale: float
    norm_ratio: float
    offset: float
    heads: int
    size: int
    feats: int
    lanes: int
    pair_feats: int
    tokens: int
    widths: tuple


def nn(left, right):
    return lax.dot_general(left, right, (((1,), (0,)), ((), ())), preferred_element_type=F32)


def nt(left, right):
    return lax.dot_general(left, right, (((1,), (1,)), ((), ())), preferred_element_type=F32)


def tn(left, right):
    return lax.dot_general(left, right, (((0,), (0,)), ((), ())), preferred_element_type=F32)


def whole(shape):
    zeros = (0,) * len(shape)
    return pl.BlockSpec(shape, lambda *_: zeros, pipeline_mode=pl.Buffered(1))


def rows_of(tile, width):
    return pl.BlockSpec((tile, width), lambda i, *_: (i, 0))


def summed(shape):
    zeros = (0,) * len(shape)
    return pl.BlockSpec(shape, lambda *_: zeros)


def shape_of(shape, dtype):
    return jax.ShapeDtypeStruct(shape, dtype)


ANY = pl.BlockSpec(memory_space=pl.ANY)


def clear(*refs):
    @pl.when(pl.program_id(0) == 0)
    def _():
        for ref in refs:
            ref[...] = jnp.zeros(ref.shape, ref.dtype)


def add_to(ref, value):
    ref[...] += value


def features(values, directions_ref, pair, consts):
    wide = values.astype(F32)
    squares = (wide * wide * consts.norm_ratio).astype(BF16)
    dots = nn(jnp.concatenate([values, squares], axis=1), directions_ref[pair])
    return jnp.exp(dots * consts.scale - consts.offset)


def live_tokens(consts, starts, lengths):
    place = lax.axis_index("seq") * consts.tokens
    count = 0
    for bucket, width in enumerate(consts.widths):
        before = place - starts[bucket]
        inside = (before >= 0) & (before < width * consts.tokens)
        count = count + jnp.where(inside, jnp.clip(lengths[bucket] - before, 0, consts.tokens), 0)
    return count


def key_kernel(consts, starts, lengths, x_ref, wk_ref, wv_ref, par_ref, turns_ref,
               k_ref, v_ref, kf_ref, sum_ref, dirs_ref, vt_ref):
    heads, size, feats, lanes, pair_feats = consts.heads, consts.size, consts.feats, consts.lanes, consts.pair_feats
    group = size + 16
    clear(sum_ref)

    @pl.when(pl.program_id(0) == 0)
    def _():
        dirs_ref[...] = jnp.zeros(dirs_ref.shape, BF16)
        minus = jnp.full((size, feats), -1.0, BF16)
        for head in range(heads):
            pair, e = divmod(head, 2)
            turned = jnp.transpose(turns_ref[head].astype(F32)).astype(BF16)
            dirs_ref[pair, pl.ds(e * size, size), pl.ds(e * feats, feats)] = turned
            dirs_ref[pair, pl.ds(lanes + e * size, size), pl.ds(e * feats, feats)] = minus

    tile = x_ref.shape[0]
    x = x_ref[...]
    k_ref[...] = (nn(x, wk_ref[...]) + par_ref[1:2]).astype(BF16)
    values = nn(x, wv_ref[...]) + par_ref[2:3]
    v_ref[...] = values.astype(BF16)
    place = lax.broadcasted_iota(jnp.int32, (group, tile), 1) + pl.program_id(0) * tile
    live = jnp.where(place < live_tokens(consts, starts, lengths), 1.0, 0.0)
    row = lax.broadcasted_iota(jnp.int32, (group - size, tile), 0)
    ones = jnp.where(row == 0, live[size:], 0.0).astype(BF16)
    turned = jnp.transpose(values)
    for head in range(heads):
        part = turned[head * size : (head + 1) * size] * live[:size]
        vt_ref[pl.ds(head * group, size), :] = part.astype(BF16)
        vt_ref[pl.ds(head * group + size, group - size), :] = ones
    for pair in range(heads // 2):
        feat = features(k_ref[:, pl.ds(pair * lanes, lanes)], dirs_ref, pair, consts).astype(BF16)
        kf_ref[:, pl.ds(pair * pair_feats, pair_feats)] = feat
        for e in range(2):
            head = 2 * pair + e
            part = nn(vt_ref[pl.ds(head * group, group), :], feat[:, e * feats : (e + 1) * feats])
            add_to(sum_ref.at[pl.ds(head * size, size), :], part[:size])
            add_to(sum_ref.at[pl.ds(heads * size + head, 1), :], part[size : size + 1])


def query_kernel(consts, x_ref, wq_ref, par_ref, dirs_ref, *rest):
    q_ref, qf_ref = rest[-2:]
    q_ref[...] = (nn(x_ref[...], wq_ref[...]) + par_ref[0:1]).astype(BF16)
    for pair in range(consts.heads // 2):
        qf_ref[:, pl.ds(pair * consts.pair_feats, consts.pair_feats)] = features(
            q_ref[:, pl.ds(pair * consts.lanes, consts.lanes)], dirs_ref, pair, consts
        ).astype(BF16)


def place_sums(consts, total_ref, sums_ref):
    heads, size, feats, lanes = consts.heads, consts.size, consts.feats, consts.lanes

    @pl.when(pl.program_id(0) == 0)
    def _():
        sums_ref[...] = jnp.zeros(sums_ref.shape, BF16)
        for head in range(heads):
            pair, e = divmod(head, 2)
            cut = pl.ds(e * feats, feats)
            sums_ref[pair, pl.ds(e * size, size), cut] = total_ref[pl.ds(head * size, size), :].astype(BF16)
            if sums_ref.shape[1] > lanes:
                row = total_ref[pl.ds(heads * size + head, 1), :]
                sums_ref[pair, pl.ds(lanes + e * size, size), cut] = jnp.broadcast_to(row, (size, feats)).astype(BF16)


def centred(hidden):
    centre = hidden - jnp.mean(hidden, axis=-1, keepdims=True)
    spread = jnp.mean(centre * centre, axis=-1, keepdims=True)
    rstd = lax.rsqrt(spread + EPSILON)
    return centre * rstd, rstd


def norm_back(grad, unit, rstd):
    return rstd * (
        grad
        - jnp.mean(grad, axis=-1, keepdims=True)
        - unit * jnp.mean(grad * unit, axis=-1, keepdims=True)
    )


def forward_kernel(consts, x_ref, ct_ref, qf_ref, total_ref, wo_ref, wu_ref, wd_ref, par_ref,
                   out_ref, mix_ref, rden_ref, unit_ref, rstd_ref, low_ref, sg_ref, fg_ref, act_ref, slope_ref,
                   small_ref, sums_ref):
    lanes, pair_feats = consts.lanes, consts.pair_feats
    clear(small_ref)
    place_sums(consts, total_ref, sums_ref)
    for pair in range(consts.heads // 2):
        both = nt(qf_ref[:, pl.ds(pair * pair_feats, pair_feats)], sums_ref[pair])
        rden = 1.0 / both[:, lanes:]
        rden_ref[:, pl.ds(pair * lanes, lanes)] = rden
        mix_ref[:, pl.ds(pair * lanes, lanes)] = (both[:, :lanes] * rden).astype(BF16)
    hidden = x_ref[...].astype(F32) + (nn(mix_ref[...], wo_ref[...]) + par_ref[3:4])
    unit, rstd = centred(hidden)
    unit_ref[...] = unit
    rstd_ref[...] = jnp.broadcast_to(rstd, rstd_ref.shape)
    normed = unit * par_ref[5:6] + par_ref[6:7]
    low_ref[...] = normed.astype(BF16)
    chunk = par_ref.shape[1]
    for part in range(wu_ref.shape[1] // chunk):
        cut = pl.ds(part * chunk, chunk)
        pre = nn(low_ref[...], wu_ref[:, cut]) + par_ref[9 + part : 10 + part]
        square = pre * pre
        gate = jnp.tanh(pre * (GELU_SCALE + (GELU_SCALE * GELU_CUBE) * square))
        half = 0.5 + 0.5 * gate
        act = pre * half
        act_ref[:, cut] = act.astype(BF16)
        slope = half + act * (1.0 - gate) * (GELU_SCALE + (3.0 * GELU_SCALE * GELU_CUBE) * square)
        slope_ref[:, cut] = slope.astype(BF16)
    hidden = normed + (nn(act_ref[...], wd_ref[...]) + par_ref[4:5])
    unit, rstd = centred(hidden)
    out_ref[...] = unit * par_ref[7:8] + par_ref[8:9]
    seed = ct_ref[...].astype(F32)
    second = norm_back(seed * par_ref[7:8], unit, rstd)
    sg_ref[...] = second
    feed = second.astype(BF16)
    fg_ref[...] = feed
    parts = [
        jnp.sum(seed * unit, axis=0, keepdims=True),
        jnp.sum(seed, axis=0, keepdims=True),
        jnp.sum(feed.astype(F32), axis=0, keepdims=True),
    ]
    for row, part in enumerate(parts):
        add_to(small_ref.at[pl.ds(row, 1), :], part)


def feed_back_kernel(chunk, fg_ref, slope_ref, sg_ref, unit_ref, rstd_ref, wu_ref, wd_ref, par_ref,
                     pg_ref, rg_ref, bg_ref, small_ref, bup_ref):
    clear(small_ref, bup_ref)
    for part in range(wu_ref.shape[1] // chunk):
        cut = pl.ds(part * chunk, chunk)
        pre_grad = nt(fg_ref[...], wd_ref[cut, :]) * slope_ref[:, cut].astype(F32)
        low = pre_grad.astype(BF16)
        pg_ref[:, cut] = low
        add_to(bup_ref.at[:, cut], jnp.sum(low.astype(F32), axis=0, keepdims=True))
    normed_grad = sg_ref[...] + nt(pg_ref[...], wu_ref[...])
    unit = unit_ref[...]
    residual = norm_back(normed_grad * par_ref[5:6], unit, rstd_ref[:, :1])
    rg_ref[...] = residual
    branch = residual.astype(BF16)
    bg_ref[...] = branch
    parts = [
        jnp.sum(normed_grad * unit, axis=0, keepdims=True),
        jnp.sum(normed_grad, axis=0, keepdims=True),
        jnp.sum(branch.astype(F32), axis=0, keepdims=True),
    ]
    for row, part in enumerate(parts):
        add_to(small_ref.at[pl.ds(row, 1), :], part)


def attention_back_kernel(consts, bg_ref, mix_ref, rden_ref, qf_ref, q_ref, sd_ref, dirs_ref, wo_ref,
                          qg_ref, sum_ref, bq_ref, gt_ref):
    heads, size, feats, lanes, pair_feats = consts.heads, consts.size, consts.feats, consts.lanes, consts.pair_feats
    clear(sum_ref, bq_ref)
    attended = nt(bg_ref[...], wo_ref[...]) * rden_ref[...]
    numerator_grad = attended.astype(BF16)
    density = -attended * mix_ref[...].astype(F32)
    density_grad = density.astype(BF16)
    turned, turned_density = jnp.transpose(attended), jnp.transpose(density)
    for head in range(heads):
        gt_ref[pl.ds(head * lanes, size), :] = turned[head * size : (head + 1) * size].astype(BF16)
        gt_ref[pl.ds(head * lanes + size, size), :] = turned_density[head * size : (head + 1) * size].astype(BF16)
    for pair in range(heads // 2):
        cut = slice(pair * lanes, (pair + 1) * lanes)
        feat = qf_ref[:, pl.ds(pair * pair_feats, pair_feats)]
        grad = nn(jnp.concatenate([numerator_grad[:, cut], density_grad[:, cut]], axis=1), sd_ref[pair])
        logit_grad = (grad * feat.astype(F32)).astype(BF16)
        through = nt(logit_grad, dirs_ref[pair])
        query = q_ref[:, pl.ds(pair * lanes, lanes)].astype(F32)
        low = (consts.scale * through[:, :lanes] + through[:, lanes:] * query * (2.0 * consts.norm_ratio * consts.scale)).astype(BF16)
        qg_ref[:, pl.ds(pair * lanes, lanes)] = low
        add_to(bq_ref.at[:, pl.ds(pair * lanes, lanes)], jnp.sum(low.astype(F32), axis=0, keepdims=True))
        for e in range(2):
            head = 2 * pair + e
            part = nn(gt_ref[pl.ds(head * lanes, lanes), :], feat[:, e * feats : (e + 1) * feats])
            add_to(sum_ref.at[pl.ds(head * size, size), :], part[:size])
            add_to(sum_ref.at[pl.ds(heads * size + head, 1), :], jnp.sum(part[size:], axis=0, keepdims=True))


def key_back_kernel(consts, starts, lengths, v_ref, k_ref, kf_ref, total_ref, dirs_ref,
                    kg_ref, vg_ref, small_ref, sg_ref):
    heads, size, feats, lanes, pair_feats = consts.heads, consts.size, consts.feats, consts.lanes, consts.pair_feats
    clear(small_ref)
    place_sums(consts, total_ref, sg_ref)
    tile = v_ref.shape[0]
    row = lax.broadcasted_iota(jnp.int32, (tile, lanes), 0) + pl.program_id(0) * tile
    live = row < live_tokens(consts, starts, lengths)
    sums = [[], []]
    for pair in range(heads // 2):
        cut = pl.ds(pair * lanes, lanes)
        feat_cut = pl.ds(pair * pair_feats, pair_feats)
        feat = kf_ref[:, feat_cut]
        base = heads * size + 2 * pair
        add = jnp.concatenate([total_ref[pl.ds(base, 1), :], total_ref[pl.ds(base + 1, 1), :]], axis=1)
        grad = nn(v_ref[:, cut], sg_ref[pair]) + add
        logit_grad = (grad * feat.astype(F32)).astype(BF16)
        through = nt(logit_grad, dirs_ref[pair])
        key = k_ref[:, cut].astype(F32)
        low = consts.scale * through[:, :lanes] + through[:, lanes:] * key * (2.0 * consts.norm_ratio * consts.scale)
        low = jnp.where(live, low, 0.0).astype(BF16)
        kg_ref[:, cut] = low
        value = jnp.where(live, nt(feat, sg_ref[pair]), 0.0).astype(BF16)
        vg_ref[:, cut] = value
        sums[0].append(jnp.sum(low.astype(F32), axis=0, keepdims=True))
        sums[1].append(jnp.sum(value.astype(F32), axis=0, keepdims=True))
    for number, part in enumerate(sums):
        add_to(small_ref.at[pl.ds(number, 1), :], jnp.concatenate(part, axis=1))


def input_kernel(first_ref, *refs):
    out_ref = refs[-1]
    total = first_ref[...]
    for grad_ref, weight_ref in zip(refs[:-1:2], refs[1:-1:2]):
        total += nt(grad_ref[...], weight_ref[...])
    out_ref[...] = total


class Order:
    def __init__(self):
        self.token = jnp.zeros((1,), jnp.int32)

    def after(self, number):
        return number + self.token[0]

    def call(self, kernel, grid, ins, outs, in_specs, out_specs, deps=(), scratch=(), prefetch=0,
             exps=0, limit=60, aliases=None):
        single = not isinstance(outs, list)
        outs, out_specs = ([outs], [out_specs]) if single else (outs, out_specs)
        given, extra = len(ins), len(deps)

        def body(*refs):
            refs[given + extra + 1 + len(outs)][0] = refs[given + extra][0]
            kernel(*refs[:given], *refs[given + extra + 1 : given + extra + 1 + len(outs)],
                   *refs[given + extra + 2 + len(outs) :])

        number = pl.BlockSpec(memory_space=pltpu.SMEM)
        *results, self.token = pl.pallas_call(
            body,
            out_shape=[*outs, shape_of((1,), jnp.int32)],
            grid_spec=pltpu.PrefetchScalarGridSpec(
                num_scalar_prefetch=prefetch,
                grid=grid,
                in_specs=[*in_specs, *[ANY] * extra, number],
                out_specs=[*out_specs, number],
                scratch_shapes=scratch,
            ),
            input_output_aliases=aliases or {},
            compiler_params=pltpu.CompilerParams(vmem_limit_bytes=limit * MIB),
            cost_estimate=pl.CostEstimate(flops=1, bytes_accessed=1, transcendentals=0),
        )(*ins, *deps, self.token)
        return results[0] if single else results


def outer_tall_kernel(start, a_ref, b_ref, out_ref):
    out_ref[0] = tn(a_ref[...], b_ref[...])


def outer_tall(order, which, a, b, deps=()):
    (tokens, rows), columns, tile = a.shape, b.shape[1], 256
    count = rows // 4 // tile
    return order.call(
        outer_tall_kernel, (2 * count,), [which.reshape(1), a, b], shape_of((2, rows // 4, columns), F32),
        [pl.BlockSpec((tokens, tile), lambda i, which: (0, which[0] * 2 * count + i)), whole(b.shape)],
        pl.BlockSpec((1, tile, columns), lambda i, which: (i // count, i % count, 0)), prefetch=1, deps=deps,
    )


def turn(a_ref, turned_ref):
    @pl.when(pl.program_id(0) == 0)
    def _():
        turned_ref[...] = jnp.transpose(a_ref[...])


def outer_flat_kernel(a_ref, b_ref, *rest):
    out_ref, turned_ref = rest[-2:]
    turn(a_ref, turned_ref)
    out_ref[...] = nn(turned_ref[...], b_ref[...])


def outer_flat(order, a, b, part, given=(), deps=()):
    (tokens, rows), columns, tile = a.shape, b.shape[1], 512
    count = columns // 2 // tile
    cut = [pl.BlockSpec((n, tile), lambda i: (0, part * count + i)) for n in (tokens, rows)]
    return order.call(
        outer_flat_kernel, (count,), [a, b, *given], shape_of((rows, columns), F32),
        [whole(a.shape), cut[0], *[ANY] * len(given)], cut[1],
        scratch=[pltpu.VMEM((rows, tokens), BF16)], deps=deps, aliases={2 + n: n for n in range(len(given))},
    )


def outer_duo_kernel(which, a0_ref, b0_ref, a1_ref, b1_ref, out_ref, turned0_ref, turned1_ref):
    turn(a0_ref, turned0_ref)
    turn(a1_ref, turned1_ref)
    out_ref[0] = nn(turned0_ref[...], b0_ref[...])
    out_ref[1] = nn(turned1_ref[...], b1_ref[...])


def outer_duo(order, which, a0, b0, a1, b1, deps=()):
    (tokens, rows), columns, tile = a0.shape, b0.shape[1], 256
    left = pl.BlockSpec((tokens, rows // 2), lambda i, which: (0, which[0]), pipeline_mode=pl.Buffered(1))
    right = pl.BlockSpec((tokens, tile), lambda i, which: (0, i))
    return order.call(
        outer_duo_kernel, (columns // tile,), [which.reshape(1), a0, b0, a1, b1],
        shape_of((2, rows // 2, columns), F32), [left, right, left, right],
        pl.BlockSpec((2, rows // 2, tile), lambda i, which: (0, 0, i)),
        scratch=[pltpu.VMEM((rows // 2, tokens), BF16)] * 2, prefetch=1, deps=deps,
    )


def part_sums(order, total, tag, before):
    lead, (rows, columns) = total.shape[:-2], total.shape[-2:]
    parted = total.reshape(*lead, before, 2, rows // (2 * before), columns)
    mine = order.after(coordinate(tag))
    cuts = [lax.dynamic_index_in_dim(parted, n, parted.ndim - 3, keepdims=False) for n in (1 - mine, mine)]
    return [part.reshape(*lead, rows // 2, columns) for part in cuts]


def bits_of(axis):
    return [(axis, bit) for bit in range(lax.axis_size(axis).bit_length() - 1)]


def coordinate(tag):
    return (lax.axis_index(tag[0]) >> tag[1]) & 1


def exchange(sent, tag):
    pairs = [(i, i ^ (1 << tag[1])) for i in range(lax.axis_size(tag[0]))]
    return lax.ppermute(sent, tag[0], pairs)


def halving(order, array, tags, sequence):
    left = list(tags)
    for tag in sequence:
        where = left.index(tag)
        mine = order.after(coordinate(tag))
        sent = lax.dynamic_index_in_dim(array, 1 - mine, where, keepdims=False)
        kept = lax.dynamic_index_in_dim(array, mine, where, keepdims=False)
        received = exchange(sent, tag)
        yield sent
        array = kept + received
        left.pop(where)
    yield array


def doubling(order, block, sequence):
    for tag in reversed(sequence):
        other = exchange(block, tag)
        yield block
        mine = order.after(coordinate(tag)) == 0
        block = jnp.stack([jnp.where(mine, block, other), jnp.where(mine, other, block)])
    yield block


def summing(order, array, sequence):
    for tag in sequence:
        other = exchange(array, tag)
        yield array
        array = array + other + order.after(0).astype(F32)
    yield array


def weight_tags():
    seq, row = bits_of("seq"), bits_of("row")
    first = seq[:1] + row + seq[1:]
    second = seq[:2] + row + seq[2:]
    return first, second


def stacked_from(place):
    first, second = weight_tags()
    return first[place:] == second[place:]


def scatter_pair(order, sent, kept):
    orders = weight_tags()
    left = [list(orders[0]), list(orders[0])]
    sent, kept = [sent], [kept]
    for place in range(len(orders[0])):
        tags = [orders[n][place] for n in range(len(kept))]
        received = [exchange(part, tag) for part, tag in zip(sent, tags)]
        for names, number in zip(left, orders):
            names.remove(number[place])
        yield sent
        totals = [stay + came for stay, came in zip(kept, received)]
        if place + 1 == len(orders[0]):
            yield totals[0] + order.after(0).astype(F32)
            return
        if stacked_from(place + 1):
            totals = totals if len(totals) == 1 else [jnp.stack(totals)]
        elif len(totals) == 1:
            totals = [totals[0][0], totals[0][1]]
        tags = [orders[n][place + 1] for n in range(len(totals))]
        befores = [1 << names.index(tag) for names, tag in zip(left, tags)]
        parts = [part_sums(order, *given) for given in zip(totals, tags, befores)]
        sent, kept = [part[0] for part in parts], [part[1] for part in parts]


def gather_pair(order, block):
    orders = weight_tags()
    held = [block]
    have = [[], []]
    for place in reversed(range(len(orders[0]))):
        if place and not stacked_from(place) and len(held) == 1:
            held = [held[0][0], held[0][1]]
        tags = [orders[n][place] for n in range(len(held))]
        others = [exchange(part, tag) for part, tag in zip(held, tags)]
        yield held
        whole_now = []
        for n, (part, other, tag) in enumerate(zip(held, others, tags)):
            mine = order.after(coordinate(tag)) == 0
            before = 1 << sum(orders[0].index(name) < orders[0].index(tag) for name in have[n])
            lead, (rows, columns) = part.shape[:-2], part.shape[-2:]
            shape = (*lead, before, rows // before, columns)
            part, other = part.reshape(shape), other.reshape(shape)
            both = jnp.stack([jnp.where(mine, part, other), jnp.where(mine, other, part)], axis=len(lead) + 1)
            whole_now.append(both.reshape(*lead, 2 * rows, columns))
        for names, number in zip(have, orders):
            names.append(number[place])
        held = whole_now
    yield held


def gather_blocks(block):
    whole = lax.all_gather(block, ("seq", "row"), axis=0, tiled=False)
    seq, row = bits_of("seq"), bits_of("row")
    tags = seq[::-1] + row[::-1]
    first, _ = weight_tags()
    whole = whole.reshape((2,) * len(tags) + block.shape)
    places = [tags.index(tag) for tag in first]
    rest = list(range(len(tags), len(tags) + block.ndim))
    return whole.transpose(places + rest)


def bucket_sum(order, onehot, shared, part):
    tags = bits_of("seq")
    padded, features = part.shape
    slots = onehot[:shared].reshape(1, shared, 1, 1)
    blocks = part.reshape(1 << len(tags), 1, padded >> len(tags), features) * slots
    blocks = blocks.reshape((2,) * len(tags) + blocks.shape[1:])
    steps = halving(order, blocks, tags, tags)
    for _ in tags:
        yield next(steps)
    steps = doubling(order, next(steps), tags)
    for _ in tags:
        yield next(steps)
    summed = next(steps)
    summed = jnp.sum(summed.reshape((1 << len(tags),) + summed.shape[len(tags) :]) * slots, axis=1)
    alone = 1.0 - jnp.sum(onehot[:shared])
    yield summed.reshape(padded, features) + alone * part


def on_device(
    inputs, w_query, w_key, w_value, w_out, w_up, w_down, b_query, b_key, b_value, b_out, b_up, b_down,
    norm1_gain, norm1_shift, norm2_gain, norm2_shift, head_feature_directions, seq_lengths, seq_starts, cotangent,
):
    tokens, width = inputs.shape[1:]
    ff = w_up.shape[1]
    heads, feats, size = head_feature_directions.shape
    pairs, lanes, pair_feats, all_feats = heads // 2, 2 * size, 2 * feats, heads * feats
    scale = size ** (-0.25)
    blocks = lax.axis_size("seq")
    widths = [5 * blocks // 8, blocks // 8] + [blocks // 16] * 4
    consts = Consts(scale, 0.5 / math.sqrt(size) / scale, 0.5 * math.log(feats), heads, size, feats, lanes, pair_feats,
                    tokens, tuple(widths))
    shared = sum(count > 1 for count in widths)
    block_start = lax.axis_index("seq") * tokens
    starts, lengths = seq_starts.reshape(-1), seq_lengths.reshape(-1)
    limits = jnp.array(widths, jnp.int32) * tokens
    onehot = ((starts <= block_start) & (block_start < starts + limits)).astype(F32)
    core = coordinate(("seq", 0))
    count = 2 * len(bits_of("seq"))
    unit = 8 << len(bits_of("seq"))
    sum_rows = -(-(width + heads) // unit) * unit

    params = jnp.concatenate(
        [b_query, b_key, b_value, b_out, b_down, norm1_gain, norm1_shift, norm2_gain, norm2_shift, b_up]
    ).astype(F32).reshape(-1, width)
    x, ct = inputs[0], cotangent[0]
    order = Order()

    def step(*parts):
        arrays = []
        for part in parts:
            given = next(part)
            arrays.extend(given if isinstance(given, list) else [given])
        return arrays

    def finish(part):
        return list(part)[-1]

    tile = 512
    steps = tokens // tile
    narrow, broad = rows_of(tile, width), rows_of(tile, all_feats)
    square, param_spec = whole((width, width)), whole(params.shape)
    sums_shape, dirs_shape = (sum_rows, feats), (pairs, 2 * lanes, pair_feats)
    dirs_spec, sums_spec, total_spec = whole(dirs_shape), whole(dirs_shape), whole(sums_shape)
    f32_rows, bf16_rows = shape_of((tokens, width), F32), shape_of((tokens, width), BF16)
    feat_rows, ff_rows = shape_of((tokens, all_feats), BF16), shape_of((tokens, ff), BF16)
    keys, values, key_feat, key_sum, dirs = order.call(
        functools.partial(key_kernel, consts), (steps,),
        [starts, lengths, x, w_key, w_value, params, head_feature_directions],
        [bf16_rows, bf16_rows, feat_rows, shape_of(sums_shape, F32), shape_of(dirs_shape, BF16)],
        [narrow, square, square, param_spec, whole(head_feature_directions.shape)],
        [narrow, narrow, broad, summed(sums_shape), summed(dirs_shape)],
        scratch=[pltpu.VMEM((heads * (size + 16), tile), BF16)], prefetch=2,
    )
    total = bucket_sum(order, onehot, shared, key_sum)

    def query_half(first, given, deps):
        cut = [pl.BlockSpec((tile, n), lambda i: (i + first, 0)) for n in (width, all_feats)]
        return order.call(
            functools.partial(query_kernel, consts), (steps // 2,),
            [x, w_query, params, dirs, *given], [bf16_rows, feat_rows],
            [cut[0], square, param_spec, dirs_spec, *[ANY] * len(given)], cut, deps=deps,
            aliases={4 + n: n for n in range(len(given))},
        )

    step(total)
    given = query_half(0, [], step(total))
    for _ in range(count - 4):
        step(total)
    queries, query_feat = query_half(steps // 2, given, step(total))
    total = finish(total)

    tile = 256
    steps = tokens // tile
    narrow, broad, long = rows_of(tile, width), rows_of(tile, all_feats), rows_of(tile, ff)
    thin = rows_of(tile, 128)
    up_spec, down_spec = whole((width, ff)), whole((ff, width))
    (result, mixture, rden, unit, rstd, normed_low, second, feed, active, slope, small_forward, sums) = order.call(
        functools.partial(forward_kernel, consts), (steps,),
        [x, ct, query_feat, total, w_out, w_up, w_down, params],
        [f32_rows, bf16_rows, f32_rows, f32_rows, shape_of((tokens, 128), F32), bf16_rows, f32_rows, bf16_rows,
         ff_rows, ff_rows, shape_of((3, width), F32), shape_of(dirs_shape, BF16)],
        [narrow, narrow, broad, total_spec, square, up_spec, down_spec, param_spec],
        [narrow, narrow, narrow, narrow, thin, narrow, narrow, narrow, long, long, summed((3, width)),
         summed(dirs_shape)],
    )

    everyone = ("seq", "row")
    down = scatter_pair(
        order, outer_tall(order, 1 - core, active, feed), outer_tall(order, core, active, feed)
    )
    step(down)
    pre_grad, residual, branch, small_back, grad_bup = order.call(
        functools.partial(feed_back_kernel, 512), (steps,),
        [feed, slope, second, unit, rstd, w_up, w_down, params],
        [ff_rows, f32_rows, bf16_rows, shape_of((3, width), F32), shape_of((1, ff), F32)],
        [narrow, long, narrow, narrow, thin, up_spec, down_spec, param_spec],
        [long, narrow, narrow, summed((3, width)), summed((1, ff))],
        deps=step(down),
    )
    query_grad, query_sum, grad_bquery = order.call(
        functools.partial(attention_back_kernel, consts), (steps,),
        [branch, mixture, rden, query_feat, queries, sums, dirs, w_out],
        [bf16_rows, shape_of(sums_shape, F32), shape_of((1, width), F32)],
        [narrow, narrow, narrow, broad, narrow, sums_spec, dirs_spec, square],
        [narrow, summed(sums_shape), summed((1, width))],
        scratch=[pltpu.VMEM((heads * lanes, tile), BF16)],
        deps=step(down),
    )
    small = jnp.concatenate([small_forward, small_back, grad_bquery, grad_bup.reshape(-1, width)])
    small = summing(order, small, weight_tags()[0])
    total = bucket_sum(order, onehot, shared, query_sum)
    step(total)
    grad_up = outer_flat(order, normed_low, pre_grad, 0, (), step(total) + step(down) + step(small))
    grad_up = outer_flat(order, normed_low, pre_grad, 1, (grad_up,), step(total) + step(down) + step(small))
    whole_up = lax.psum(grad_up, everyone)
    down = gather_blocks(finish(down))
    first_sent = outer_duo(order, 1 - core, mixture, branch, x, query_grad, step(total) + step(small))
    first_kept = outer_duo(order, core, mixture, branch, x, query_grad, step(total) + step(small))
    first = scatter_pair(order, first_sent, first_kept)
    step(first)
    for _ in range(count - 7):
        step(total)

    tile = 512
    steps = tokens // tile
    narrow, broad = rows_of(tile, width), rows_of(tile, all_feats)
    partial_input = order.call(
        input_kernel, (steps,), [residual, query_grad, w_query], f32_rows, [narrow, narrow, square], narrow,
        deps=step(total) + step(first) + step(small),
    )
    small = finish(small)
    total = finish(total)
    key_grad, value_grad, small_key = order.call(
        functools.partial(key_back_kernel, consts), (steps,),
        [starts, lengths, values, keys, key_feat, total, dirs],
        [bf16_rows, bf16_rows, shape_of((2, width), F32)],
        [narrow, narrow, broad, total_spec, dirs_spec],
        [narrow, narrow, summed((2, width))], prefetch=2,
        scratch=[pltpu.VMEM((pairs, lanes, pair_feats), BF16)],
        deps=step(first),
    )
    late = summing(order, small_key, weight_tags()[0])
    last_sent = outer_duo(order, 1 - core, x, key_grad, x, value_grad, step(first) + step(late))
    last_kept = outer_duo(order, core, x, key_grad, x, value_grad, step(first) + step(late))
    first = gather_pair(order, finish(first))
    last = scatter_pair(order, last_sent, last_kept)
    step(last)
    input_grad = order.call(
        input_kernel, (steps,), [partial_input, key_grad, w_key, value_grad, w_value], f32_rows,
        [narrow, narrow, square, narrow, square], narrow,
        deps=step(first) + step(last) + step(late),
    )
    last = gather_pair(order, finish(last))
    first, last, late = [finish(part) for part in (first, last, late)]
    first, last = [[chunk.reshape(width, width) for chunk in pair] for pair in
                   [pair if len(pair) == 2 else [pair[0][0], pair[0][1]] for pair in (first, last)]]

    bits = down.ndim - 3
    whole_down = jnp.moveaxis(down, bits, 1).reshape(ff, width)
    return (
        result[None], input_grad[None],
        first[1], last[0], last[1], first[0],
        whole_up, whole_down,
        small[6], late[0], late[1], small[5], small[7:].reshape(ff), small[2],
        small[3], small[4], small[0], small[1],
    )


def solution(mesh):
    tokens = P("row", "seq", None)
    bucket = P("row", None)
    return jax.shard_map(
        on_device,
        mesh=mesh,
        in_specs=(tokens,) + (P(),) * 17 + (bucket, bucket, tokens),
        out_specs=(tokens, tokens) + (P(),) * 16,
        check_vma=False,
    )
```

```python
import functools
import math
import typing

import jax
import jax.numpy as jnp
from jax import lax
from jax.experimental import pallas as pl
from jax.experimental.pallas import tpu as pltpu
from jax.sharding import PartitionSpec as P

EPSILON = 1e-05
F32, BF16 = jnp.float32, jnp.bfloat16
MIB = 1 << 20
GELU_SCALE = math.sqrt(2.0 / math.pi)
GELU_CUBE = 0.044715


class Consts(typing.NamedTuple):
    scale: float
    norm_ratio: float
    offset: float
    heads: int
    size: int
    feats: int
    lanes: int
    pair_feats: int
    tokens: int
    widths: tuple


def nn(left, right):
    return lax.dot_general(left, right, (((1,), (0,)), ((), ())), preferred_element_type=F32)


def nt(left, right):
    return lax.dot_general(left, right, (((1,), (1,)), ((), ())), preferred_element_type=F32)


def tn(left, right):
    return lax.dot_general(left, right, (((0,), (0,)), ((), ())), preferred_element_type=F32)


def whole(shape):
    zeros = (0,) * len(shape)
    return pl.BlockSpec(shape, lambda *_: zeros, pipeline_mode=pl.Buffered(1))


def rows_of(tile, width):
    return pl.BlockSpec((tile, width), lambda i, *_: (i, 0))


def summed(shape):
    zeros = (0,) * len(shape)
    return pl.BlockSpec(shape, lambda *_: zeros)


def shape_of(shape, dtype):
    return jax.ShapeDtypeStruct(shape, dtype)


ANY = pl.BlockSpec(memory_space=pl.ANY)


def clear(*refs):
    @pl.when(pl.program_id(0) == 0)
    def _():
        for ref in refs:
            ref[...] = jnp.zeros(ref.shape, ref.dtype)


def add_to(ref, value):
    ref[...] += value


def features(values, directions_ref, pair, consts):
    wide = values.astype(F32)
    squares = (wide * wide * consts.norm_ratio).astype(BF16)
    dots = nn(jnp.concatenate([values, squares], axis=1), directions_ref[pair])
    return jnp.exp(dots * consts.scale - consts.offset)


def live_tokens(consts, starts, lengths):
    place = lax.axis_index("seq") * consts.tokens
    count = 0
    for bucket, width in enumerate(consts.widths):
        before = place - starts[bucket]
        inside = (before >= 0) & (before < width * consts.tokens)
        count = count + jnp.where(inside, jnp.clip(lengths[bucket] - before, 0, consts.tokens), 0)
    return count


def key_kernel(consts, starts, lengths, x_ref, wk_ref, wv_ref, par_ref, turns_ref,
               k_ref, v_ref, kf_ref, sum_ref, dirs_ref, vt_ref):
    heads, size, feats, lanes, pair_feats = consts.heads, consts.size, consts.feats, consts.lanes, consts.pair_feats
    group = size + 16
    clear(sum_ref)

    @pl.when(pl.program_id(0) == 0)
    def _():
        dirs_ref[...] = jnp.zeros(dirs_ref.shape, BF16)
        minus = jnp.full((size, feats), -1.0, BF16)
        for head in range(heads):
            pair, e = divmod(head, 2)
            dirs_ref[pair, pl.ds(e * size, size), pl.ds(e * feats, feats)] = turns_ref[head]
            dirs_ref[pair, pl.ds(lanes + e * size, size), pl.ds(e * feats, feats)] = minus

    tile = x_ref.shape[0]
    x = x_ref[...]
    k_ref[...] = (nn(x, wk_ref[...]) + par_ref[1:2]).astype(BF16)
    values = nn(x, wv_ref[...]) + par_ref[2:3]
    v_ref[...] = values.astype(BF16)
    place = lax.broadcasted_iota(jnp.int32, (group, tile), 1) + pl.program_id(0) * tile
    live = jnp.where(place < live_tokens(consts, starts, lengths), 1.0, 0.0)
    row = lax.broadcasted_iota(jnp.int32, (group - size, tile), 0)
    ones = jnp.where(row == 0, live[size:], 0.0).astype(BF16)
    turned = jnp.transpose(values)
    for head in range(heads):
        part = turned[head * size : (head + 1) * size] * live[:size]
        vt_ref[pl.ds(head * group, size), :] = part.astype(BF16)
        vt_ref[pl.ds(head * group + size, group - size), :] = ones
    for pair in range(heads // 2):
        feat = features(k_ref[:, pl.ds(pair * lanes, lanes)], dirs_ref, pair, consts).astype(BF16)
        kf_ref[:, pl.ds(pair * pair_feats, pair_feats)] = feat
        for e in range(2):
            head = 2 * pair + e
            part = nn(vt_ref[pl.ds(head * group, group), :], feat[:, e * feats : (e + 1) * feats])
            add_to(sum_ref.at[pl.ds(head * size, size), :], part[:size])
            add_to(sum_ref.at[pl.ds(heads * size + head, 1), :], part[size : size + 1])


def query_kernel(consts, x_ref, wq_ref, par_ref, dirs_ref, *rest):
    q_ref, qf_ref = rest[-2:]
    q_ref[...] = (nn(x_ref[...], wq_ref[...]) + par_ref[0:1]).astype(BF16)
    for pair in range(consts.heads // 2):
        qf_ref[:, pl.ds(pair * consts.pair_feats, consts.pair_feats)] = features(
            q_ref[:, pl.ds(pair * consts.lanes, consts.lanes)], dirs_ref, pair, consts
        ).astype(BF16)


def place_sums(consts, total_ref, sums_ref):
    heads, size, feats, lanes = consts.heads, consts.size, consts.feats, consts.lanes

    @pl.when(pl.program_id(0) == 0)
    def _():
        sums_ref[...] = jnp.zeros(sums_ref.shape, BF16)
        for head in range(heads):
            pair, e = divmod(head, 2)
            cut = pl.ds(e * feats, feats)
            sums_ref[pair, pl.ds(e * size, size), cut] = total_ref[pl.ds(head * size, size), :].astype(BF16)
            if sums_ref.shape[1] > lanes:
                row = total_ref[pl.ds(heads * size + head, 1), :]
                sums_ref[pair, pl.ds(lanes + e * size, size), cut] = jnp.broadcast_to(row, (size, feats)).astype(BF16)


def centred(hidden):
    centre = hidden - jnp.mean(hidden, axis=-1, keepdims=True)
    spread = jnp.mean(centre * centre, axis=-1, keepdims=True)
    rstd = lax.rsqrt(spread + EPSILON)
    return centre * rstd, rstd


def norm_back(grad, unit, rstd):
    return rstd * (
        grad
        - jnp.mean(grad, axis=-1, keepdims=True)
        - unit * jnp.mean(grad * unit, axis=-1, keepdims=True)
    )


def forward_kernel(consts, x_ref, ct_ref, qf_ref, total_ref, wo_ref, wu_ref, wd_ref, par_ref,
                   out_ref, mix_ref, rden_ref, unit_ref, rstd_ref, low_ref, sg_ref, fg_ref, act_ref, slope_ref,
                   small_ref, sums_ref):
    lanes, pair_feats = consts.lanes, consts.pair_feats
    clear(small_ref)
    place_sums(consts, total_ref, sums_ref)
    for pair in range(consts.heads // 2):
        both = nt(qf_ref[:, pl.ds(pair * pair_feats, pair_feats)], sums_ref[pair])
        rden = 1.0 / both[:, lanes:]
        rden_ref[:, pl.ds(pair * lanes, lanes)] = rden
        mix_ref[:, pl.ds(pair * lanes, lanes)] = (both[:, :lanes] * rden).astype(BF16)
    hidden = x_ref[...].astype(F32) + (nn(mix_ref[...], wo_ref[...]) + par_ref[3:4])
    unit, rstd = centred(hidden)
    unit_ref[...] = unit
    rstd_ref[...] = jnp.broadcast_to(rstd, rstd_ref.shape)
    normed = unit * par_ref[5:6] + par_ref[6:7]
    low_ref[...] = normed.astype(BF16)
    chunk = par_ref.shape[1]
    for part in range(wu_ref.shape[1] // chunk):
        cut = pl.ds(part * chunk, chunk)
        pre = nn(low_ref[...], wu_ref[:, cut]) + par_ref[9 + part : 10 + part]
        square = pre * pre
        gate = jnp.tanh(pre * (GELU_SCALE + (GELU_SCALE * GELU_CUBE) * square))
        half = 0.5 + 0.5 * gate
        act = pre * half
        act_ref[:, cut] = act.astype(BF16)
        slope = half + act * (1.0 - gate) * (GELU_SCALE + (3.0 * GELU_SCALE * GELU_CUBE) * square)
        slope_ref[:, cut] = slope.astype(BF16)
    hidden = normed + (nn(act_ref[...], wd_ref[...]) + par_ref[4:5])
    unit, rstd = centred(hidden)
    out_ref[...] = unit * par_ref[7:8] + par_ref[8:9]
    seed = ct_ref[...].astype(F32)
    second = norm_back(seed * par_ref[7:8], unit, rstd)
    sg_ref[...] = second
    feed = second.astype(BF16)
    fg_ref[...] = feed
    parts = [
        jnp.sum(seed * unit, axis=0, keepdims=True),
        jnp.sum(seed, axis=0, keepdims=True),
        jnp.sum(feed.astype(F32), axis=0, keepdims=True),
    ]
    for row, part in enumerate(parts):
        add_to(small_ref.at[pl.ds(row, 1), :], part)


def feed_back_kernel(chunk, fg_ref, slope_ref, sg_ref, unit_ref, rstd_ref, wu_ref, wd_ref, par_ref,
                     pg_ref, rg_ref, bg_ref, small_ref, bup_ref):
    clear(small_ref, bup_ref)
    for part in range(wu_ref.shape[1] // chunk):
        cut = pl.ds(part * chunk, chunk)
        pre_grad = nt(fg_ref[...], wd_ref[cut, :]) * slope_ref[:, cut].astype(F32)
        low = pre_grad.astype(BF16)
        pg_ref[:, cut] = low
        add_to(bup_ref.at[:, cut], jnp.sum(low.astype(F32), axis=0, keepdims=True))
    normed_grad = sg_ref[...] + nt(pg_ref[...], wu_ref[...])
    unit = unit_ref[...]
    residual = norm_back(normed_grad * par_ref[5:6], unit, rstd_ref[:, :1])
    rg_ref[...] = residual
    branch = residual.astype(BF16)
    bg_ref[...] = branch
    parts = [
        jnp.sum(normed_grad * unit, axis=0, keepdims=True),
        jnp.sum(normed_grad, axis=0, keepdims=True),
        jnp.sum(branch.astype(F32), axis=0, keepdims=True),
    ]
    for row, part in enumerate(parts):
        add_to(small_ref.at[pl.ds(row, 1), :], part)


def attention_back_kernel(consts, bg_ref, mix_ref, rden_ref, qf_ref, q_ref, sd_ref, dirs_ref, wo_ref,
                          qg_ref, sum_ref, bq_ref, gt_ref):
    heads, size, feats, lanes, pair_feats = consts.heads, consts.size, consts.feats, consts.lanes, consts.pair_feats
    clear(sum_ref, bq_ref)
    attended = nt(bg_ref[...], wo_ref[...]) * rden_ref[...]
    numerator_grad = attended.astype(BF16)
    density = -attended * mix_ref[...].astype(F32)
    density_grad = density.astype(BF16)
    turned, turned_density = jnp.transpose(attended), jnp.transpose(density)
    for head in range(heads):
        gt_ref[pl.ds(head * lanes, size), :] = turned[head * size : (head + 1) * size].astype(BF16)
        gt_ref[pl.ds(head * lanes + size, size), :] = turned_density[head * size : (head + 1) * size].astype(BF16)
    for pair in range(heads // 2):
        cut = slice(pair * lanes, (pair + 1) * lanes)
        feat = qf_ref[:, pl.ds(pair * pair_feats, pair_feats)]
        grad = nn(jnp.concatenate([numerator_grad[:, cut], density_grad[:, cut]], axis=1), sd_ref[pair])
        logit_grad = (grad * feat.astype(F32)).astype(BF16)
        through = nt(logit_grad, dirs_ref[pair])
        query = q_ref[:, pl.ds(pair * lanes, lanes)].astype(F32)
        low = (consts.scale * through[:, :lanes] + through[:, lanes:] * query * (2.0 * consts.norm_ratio * consts.scale)).astype(BF16)
        qg_ref[:, pl.ds(pair * lanes, lanes)] = low
        add_to(bq_ref.at[:, pl.ds(pair * lanes, lanes)], jnp.sum(low.astype(F32), axis=0, keepdims=True))
        for e in range(2):
            head = 2 * pair + e
            part = nn(gt_ref[pl.ds(head * lanes, lanes), :], feat[:, e * feats : (e + 1) * feats])
            add_to(sum_ref.at[pl.ds(head * size, size), :], part[:size])
            add_to(sum_ref.at[pl.ds(heads * size + head, 1), :], jnp.sum(part[size:], axis=0, keepdims=True))


def key_back_kernel(consts, starts, lengths, v_ref, k_ref, kf_ref, total_ref, dirs_ref,
                    kg_ref, vg_ref, small_ref, sg_ref):
    heads, size, feats, lanes, pair_feats = consts.heads, consts.size, consts.feats, consts.lanes, consts.pair_feats
    clear(small_ref)
    place_sums(consts, total_ref, sg_ref)
    tile = v_ref.shape[0]
    row = lax.broadcasted_iota(jnp.int32, (tile, lanes), 0) + pl.program_id(0) * tile
    live = row < live_tokens(consts, starts, lengths)
    sums = [[], []]
    for pair in range(heads // 2):
        cut = pl.ds(pair * lanes, lanes)
        feat_cut = pl.ds(pair * pair_feats, pair_feats)
        feat = kf_ref[:, feat_cut]
        base = heads * size + 2 * pair
        add = jnp.concatenate([total_ref[pl.ds(base, 1), :], total_ref[pl.ds(base + 1, 1), :]], axis=1)
        grad = nn(v_ref[:, cut], sg_ref[pair]) + add
        logit_grad = (grad * feat.astype(F32)).astype(BF16)
        through = nt(logit_grad, dirs_ref[pair])
        key = k_ref[:, cut].astype(F32)
        low = consts.scale * through[:, :lanes] + through[:, lanes:] * key * (2.0 * consts.norm_ratio * consts.scale)
        low = jnp.where(live, low, 0.0).astype(BF16)
        kg_ref[:, cut] = low
        value = jnp.where(live, nt(feat, sg_ref[pair]), 0.0).astype(BF16)
        vg_ref[:, cut] = value
        sums[0].append(jnp.sum(low.astype(F32), axis=0, keepdims=True))
        sums[1].append(jnp.sum(value.astype(F32), axis=0, keepdims=True))
    for number, part in enumerate(sums):
        add_to(small_ref.at[pl.ds(number, 1), :], jnp.concatenate(part, axis=1))


def input_kernel(first_ref, *refs):
    out_ref = refs[-1]
    total = first_ref[...]
    for grad_ref, weight_ref in zip(refs[:-1:2], refs[1:-1:2]):
        total += nt(grad_ref[...], weight_ref[...])
    out_ref[...] = total


class Order:
    def __init__(self):
        self.token = jnp.zeros((1,), jnp.int32)

    def after(self, number):
        return number + self.token[0]

    def call(self, kernel, grid, ins, outs, in_specs, out_specs, deps=(), scratch=(), prefetch=0,
             exps=0, limit=60, aliases=None):
        single = not isinstance(outs, list)
        outs, out_specs = ([outs], [out_specs]) if single else (outs, out_specs)
        given, extra = len(ins), len(deps)

        def body(*refs):
            refs[given + extra + 1 + len(outs)][0] = refs[given + extra][0]
            kernel(*refs[:given], *refs[given + extra + 1 : given + extra + 1 + len(outs)],
                   *refs[given + extra + 2 + len(outs) :])

        number = pl.BlockSpec(memory_space=pltpu.SMEM)
        *results, self.token = pl.pallas_call(
            body,
            out_shape=[*outs, shape_of((1,), jnp.int32)],
            grid_spec=pltpu.PrefetchScalarGridSpec(
                num_scalar_prefetch=prefetch,
                grid=grid,
                in_specs=[*in_specs, *[ANY] * extra, number],
                out_specs=[*out_specs, number],
                scratch_shapes=scratch,
            ),
            input_output_aliases=aliases or {},
            compiler_params=pltpu.CompilerParams(vmem_limit_bytes=limit * MIB),
            cost_estimate=pl.CostEstimate(flops=1, bytes_accessed=1, transcendentals=0),
        )(*ins, *deps, self.token)
        return results[0] if single else results


def outer_tall_kernel(start, a_ref, b_ref, out_ref):
    out_ref[0] = tn(a_ref[...], b_ref[...])


def outer_tall(order, which, a, b, deps=()):
    (tokens, rows), columns, tile = a.shape, b.shape[1], 256
    count = rows // 4 // tile
    return order.call(
        outer_tall_kernel, (2 * count,), [which.reshape(1), a, b], shape_of((2, rows // 4, columns), F32),
        [pl.BlockSpec((tokens, tile), lambda i, which: (0, which[0] * 2 * count + i)), whole(b.shape)],
        pl.BlockSpec((1, tile, columns), lambda i, which: (i // count, i % count, 0)), prefetch=1, deps=deps,
    )


def turn(a_ref, turned_ref):
    @pl.when(pl.program_id(0) == 0)
    def _():
        turned_ref[...] = jnp.transpose(a_ref[...])


def outer_flat_kernel(a_ref, b_ref, *rest):
    out_ref, turned_ref = rest[-2:]
    turn(a_ref, turned_ref)
    out_ref[...] = nn(turned_ref[...], b_ref[...])


def outer_flat(order, a, b, part, given=(), deps=()):
    (tokens, rows), columns, tile = a.shape, b.shape[1], 512
    count = columns // 2 // tile
    cut = [pl.BlockSpec((n, tile), lambda i: (0, part * count + i)) for n in (tokens, rows)]
    return order.call(
        outer_flat_kernel, (count,), [a, b, *given], shape_of((rows, columns), F32),
        [whole(a.shape), cut[0], *[ANY] * len(given)], cut[1],
        scratch=[pltpu.VMEM((rows, tokens), BF16)], deps=deps, aliases={2 + n: n for n in range(len(given))},
    )


def outer_duo_kernel(which, a0_ref, b0_ref, a1_ref, b1_ref, out_ref, turned0_ref, turned1_ref):
    turn(a0_ref, turned0_ref)
    turn(a1_ref, turned1_ref)
    out_ref[0] = nn(turned0_ref[...], b0_ref[...])
    out_ref[1] = nn(turned1_ref[...], b1_ref[...])


def outer_duo(order, which, a0, b0, a1, b1, deps=()):
    (tokens, rows), columns, tile = a0.shape, b0.shape[1], 256
    left = pl.BlockSpec((tokens, rows // 2), lambda i, which: (0, which[0]), pipeline_mode=pl.Buffered(1))
    right = pl.BlockSpec((tokens, tile), lambda i, which: (0, i))
    return order.call(
        outer_duo_kernel, (columns // tile,), [which.reshape(1), a0, b0, a1, b1],
        shape_of((2, rows // 2, columns), F32), [left, right, left, right],
        pl.BlockSpec((2, rows // 2, tile), lambda i, which: (0, 0, i)),
        scratch=[pltpu.VMEM((rows // 2, tokens), BF16)] * 2, prefetch=1, deps=deps,
    )


def part_sums(order, total, tag, before):
    lead, (rows, columns) = total.shape[:-2], total.shape[-2:]
    parted = total.reshape(*lead, before, 2, rows // (2 * before), columns)
    mine = order.after(coordinate(tag))
    cuts = [lax.dynamic_index_in_dim(parted, n, parted.ndim - 3, keepdims=False) for n in (1 - mine, mine)]
    return [part.reshape(*lead, rows // 2, columns) for part in cuts]


def bits_of(axis):
    return [(axis, bit) for bit in range(lax.axis_size(axis).bit_length() - 1)]


def coordinate(tag):
    return (lax.axis_index(tag[0]) >> tag[1]) & 1


def exchange(sent, tag):
    pairs = [(i, i ^ (1 << tag[1])) for i in range(lax.axis_size(tag[0]))]
    return lax.ppermute(sent, tag[0], pairs)


def halving(order, array, tags, sequence):
    left = list(tags)
    for tag in sequence:
        where = left.index(tag)
        mine = order.after(coordinate(tag))
        sent = lax.dynamic_index_in_dim(array, 1 - mine, where, keepdims=False)
        kept = lax.dynamic_index_in_dim(array, mine, where, keepdims=False)
        received = exchange(sent, tag)
        yield sent
        array = kept + received
        left.pop(where)
    yield array


def doubling(order, block, sequence):
    for tag in reversed(sequence):
        other = exchange(block, tag)
        yield block
        mine = order.after(coordinate(tag)) == 0
        block = jnp.stack([jnp.where(mine, block, other), jnp.where(mine, other, block)])
    yield block


def summing(order, array, sequence):
    for tag in sequence:
        other = exchange(array, tag)
        yield array
        array = array + other + order.after(0).astype(F32)
    yield array


def weight_tags():
    seq, row = bits_of("seq"), bits_of("row")
    first = seq[:1] + row + seq[1:]
    second = seq[:2] + row + seq[2:]
    return first, second


def stacked_from(place):
    first, second = weight_tags()
    return first[place:] == second[place:]


def scatter_pair(order, sent, kept):
    orders = weight_tags()
    left = [list(orders[0]), list(orders[0])]
    sent, kept = [sent], [kept]
    for place in range(len(orders[0])):
        tags = [orders[n][place] for n in range(len(kept))]
        received = [exchange(part, tag) for part, tag in zip(sent, tags)]
        for names, number in zip(left, orders):
            names.remove(number[place])
        yield sent
        totals = [stay + came for stay, came in zip(kept, received)]
        if place + 1 == len(orders[0]):
            yield totals[0] + order.after(0).astype(F32)
            return
        if stacked_from(place + 1):
            totals = totals if len(totals) == 1 else [jnp.stack(totals)]
        elif len(totals) == 1:
            totals = [totals[0][0], totals[0][1]]
        tags = [orders[n][place + 1] for n in range(len(totals))]
        befores = [1 << names.index(tag) for names, tag in zip(left, tags)]
        parts = [part_sums(order, *given) for given in zip(totals, tags, befores)]
        sent, kept = [part[0] for part in parts], [part[1] for part in parts]


def gather_pair(order, block):
    orders = weight_tags()
    held = [block]
    have = [[], []]
    for place in reversed(range(len(orders[0]))):
        if place and not stacked_from(place) and len(held) == 1:
            held = [held[0][0], held[0][1]]
        tags = [orders[n][place] for n in range(len(held))]
        others = [exchange(part, tag) for part, tag in zip(held, tags)]
        yield held
        whole_now = []
        for n, (part, other, tag) in enumerate(zip(held, others, tags)):
            mine = order.after(coordinate(tag)) == 0
            before = 1 << sum(orders[0].index(name) < orders[0].index(tag) for name in have[n])
            lead, (rows, columns) = part.shape[:-2], part.shape[-2:]
            shape = (*lead, before, rows // before, columns)
            part, other = part.reshape(shape), other.reshape(shape)
            both = jnp.stack([jnp.where(mine, part, other), jnp.where(mine, other, part)], axis=len(lead) + 1)
            whole_now.append(both.reshape(*lead, 2 * rows, columns))
        for names, number in zip(have, orders):
            names.append(number[place])
        held = whole_now
    yield held


def gather_blocks(block):
    whole = lax.all_gather(block, ("seq", "row"), axis=0, tiled=False)
    seq, row = bits_of("seq"), bits_of("row")
    tags = seq[::-1] + row[::-1]
    first, _ = weight_tags()
    whole = whole.reshape((2,) * len(tags) + block.shape)
    places = [tags.index(tag) for tag in first]
    rest = list(range(len(tags), len(tags) + block.ndim))
    return whole.transpose(places + rest)


def bucket_sum(order, onehot, shared, part):
    tags = bits_of("seq")
    padded, features = part.shape
    slots = onehot[:shared].reshape(1, shared, 1, 1)
    blocks = part.reshape(1 << len(tags), 1, padded >> len(tags), features) * slots
    blocks = blocks.reshape((2,) * len(tags) + blocks.shape[1:])
    steps = halving(order, blocks, tags, tags)
    for _ in tags:
        yield next(steps)
    steps = doubling(order, next(steps), tags)
    for _ in tags:
        yield next(steps)
    summed = next(steps)
    summed = jnp.sum(summed.reshape((1 << len(tags),) + summed.shape[len(tags) :]) * slots, axis=1)
    alone = 1.0 - jnp.sum(onehot[:shared])
    yield summed.reshape(padded, features) + alone * part


def on_device(
    inputs, w_query, w_key, w_value, w_out, w_up, w_down, b_query, b_key, b_value, b_out, b_up, b_down,
    norm1_gain, norm1_shift, norm2_gain, norm2_shift, head_feature_directions, seq_lengths, seq_starts, cotangent,
):
    tokens, width = inputs.shape[1:]
    ff = w_up.shape[1]
    heads, feats, size = head_feature_directions.shape
    pairs, lanes, pair_feats, all_feats = heads // 2, 2 * size, 2 * feats, heads * feats
    scale = size ** (-0.25)
    blocks = lax.axis_size("seq")
    widths = [5 * blocks // 8, blocks // 8] + [blocks // 16] * 4
    consts = Consts(scale, 0.5 / math.sqrt(size) / scale, 0.5 * math.log(feats), heads, size, feats, lanes, pair_feats,
                    tokens, tuple(widths))
    shared = sum(count > 1 for count in widths)
    block_start = lax.axis_index("seq") * tokens
    starts, lengths = seq_starts.reshape(-1), seq_lengths.reshape(-1)
    limits = jnp.array(widths, jnp.int32) * tokens
    onehot = ((starts <= block_start) & (block_start < starts + limits)).astype(F32)
    core = coordinate(("seq", 0))
    count = 2 * len(bits_of("seq"))
    unit = 8 << len(bits_of("seq"))
    sum_rows = -(-(width + heads) // unit) * unit

    vectors = [b_query, b_key, b_value, b_out, b_down, norm1_gain, norm1_shift, norm2_gain, norm2_shift, b_up]
    params = jnp.concatenate([vector.astype(F32).reshape(-1, width) for vector in vectors])
    turns = head_feature_directions.transpose(0, 2, 1)
    x, ct = inputs[0], cotangent[0]
    order = Order()

    def step(*parts):
        arrays = []
        for part in parts:
            given = next(part)
            arrays.extend(given if isinstance(given, list) else [given])
        return arrays

    def finish(part):
        return list(part)[-1]

    tile = 512
    steps = tokens // tile
    narrow, broad = rows_of(tile, width), rows_of(tile, all_feats)
    square, param_spec = whole((width, width)), whole(params.shape)
    sums_shape, dirs_shape = (sum_rows, feats), (pairs, 2 * lanes, pair_feats)
    dirs_spec, sums_spec, total_spec = whole(dirs_shape), whole(dirs_shape), whole(sums_shape)
    f32_rows, bf16_rows = shape_of((tokens, width), F32), shape_of((tokens, width), BF16)
    feat_rows, ff_rows = shape_of((tokens, all_feats), BF16), shape_of((tokens, ff), BF16)
    keys, values, key_feat, key_sum, dirs = order.call(
        functools.partial(key_kernel, consts), (steps,),
        [starts, lengths, x, w_key, w_value, params, turns],
        [bf16_rows, bf16_rows, feat_rows, shape_of(sums_shape, F32), shape_of(dirs_shape, BF16)],
        [narrow, square, square, param_spec, whole(turns.shape)],
        [narrow, narrow, broad, summed(sums_shape), summed(dirs_shape)],
        scratch=[pltpu.VMEM((heads * (size + 16), tile), BF16)], prefetch=2,
    )
    total = bucket_sum(order, onehot, shared, key_sum)

    def query_half(first, given, deps):
        cut = [pl.BlockSpec((tile, n), lambda i: (i + first, 0)) for n in (width, all_feats)]
        return order.call(
            functools.partial(query_kernel, consts), (steps // 2,),
            [x, w_query, params, dirs, *given], [bf16_rows, feat_rows],
            [cut[0], square, param_spec, dirs_spec, *[ANY] * len(given)], cut, deps=deps,
            aliases={4 + n: n for n in range(len(given))},
        )

    step(total)
    given = query_half(0, [], step(total))
    for _ in range(count - 4):
        step(total)
    queries, query_feat = query_half(steps // 2, given, step(total))
    total = finish(total)

    tile = 256
    steps = tokens // tile
    narrow, broad, long = rows_of(tile, width), rows_of(tile, all_feats), rows_of(tile, ff)
    thin = rows_of(tile, 128)
    up_spec, down_spec = whole((width, ff)), whole((ff, width))
    (result, mixture, rden, unit, rstd, normed_low, second, feed, active, slope, small_forward, sums) = order.call(
        functools.partial(forward_kernel, consts), (steps,),
        [x, ct, query_feat, total, w_out, w_up, w_down, params],
        [f32_rows, bf16_rows, f32_rows, f32_rows, shape_of((tokens, 128), F32), bf16_rows, f32_rows, bf16_rows,
         ff_rows, ff_rows, shape_of((3, width), F32), shape_of(dirs_shape, BF16)],
        [narrow, narrow, broad, total_spec, square, up_spec, down_spec, param_spec],
        [narrow, narrow, narrow, narrow, thin, narrow, narrow, narrow, long, long, summed((3, width)),
         summed(dirs_shape)],
    )

    everyone = ("seq", "row")
    down = scatter_pair(
        order, outer_tall(order, 1 - core, active, feed), outer_tall(order, core, active, feed)
    )
    step(down)
    pre_grad, residual, branch, small_back, grad_bup = order.call(
        functools.partial(feed_back_kernel, 512), (steps,),
        [feed, slope, second, unit, rstd, w_up, w_down, params],
        [ff_rows, f32_rows, bf16_rows, shape_of((3, width), F32), shape_of((1, ff), F32)],
        [narrow, long, narrow, narrow, thin, up_spec, down_spec, param_spec],
        [long, narrow, narrow, summed((3, width)), summed((1, ff))],
        deps=step(down),
    )
    query_grad, query_sum, grad_bquery = order.call(
        functools.partial(attention_back_kernel, consts), (steps,),
        [branch, mixture, rden, query_feat, queries, sums, dirs, w_out],
        [bf16_rows, shape_of(sums_shape, F32), shape_of((1, width), F32)],
        [narrow, narrow, narrow, broad, narrow, sums_spec, dirs_spec, square],
        [narrow, summed(sums_shape), summed((1, width))],
        scratch=[pltpu.VMEM((heads * lanes, tile), BF16)],
        deps=step(down),
    )
    small = jnp.concatenate([small_forward, small_back, grad_bquery, grad_bup.reshape(-1, width)])
    small = summing(order, small, weight_tags()[0])
    total = bucket_sum(order, onehot, shared, query_sum)
    step(total)
    grad_up = outer_flat(order, normed_low, pre_grad, 0, (), step(total) + step(down) + step(small))
    grad_up = outer_flat(order, normed_low, pre_grad, 1, (grad_up,), step(total) + step(down) + step(small))
    whole_up = lax.psum(grad_up, everyone)
    down = gather_blocks(finish(down))
    first_sent = outer_duo(order, 1 - core, mixture, branch, x, query_grad, step(total) + step(small))
    first_kept = outer_duo(order, core, mixture, branch, x, query_grad, step(total) + step(small))
    first = scatter_pair(order, first_sent, first_kept)
    step(first)
    for _ in range(count - 7):
        step(total)

    tile = 512
    steps = tokens // tile
    narrow, broad = rows_of(tile, width), rows_of(tile, all_feats)
    partial_input = order.call(
        input_kernel, (steps,), [residual, query_grad, w_query], f32_rows, [narrow, narrow, square], narrow,
        deps=step(total) + step(first) + step(small),
    )
    small = finish(small)
    total = finish(total)
    key_grad, value_grad, small_key = order.call(
        functools.partial(key_back_kernel, consts), (steps,),
        [starts, lengths, values, keys, key_feat, total, dirs],
        [bf16_rows, bf16_rows, shape_of((2, width), F32)],
        [narrow, narrow, broad, total_spec, dirs_spec],
        [narrow, narrow, summed((2, width))], prefetch=2,
        scratch=[pltpu.VMEM((pairs, lanes, pair_feats), BF16)],
        deps=step(first),
    )
    late = summing(order, small_key, weight_tags()[0])
    last_sent = outer_duo(order, 1 - core, x, key_grad, x, value_grad, step(first) + step(late))
    last_kept = outer_duo(order, core, x, key_grad, x, value_grad, step(first) + step(late))
    first = gather_pair(order, finish(first))
    last = scatter_pair(order, last_sent, last_kept)
    step(last)
    step(first, last)
    step(first, last)
    input_grad = order.call(
        input_kernel, (steps,), [partial_input, key_grad, w_key, value_grad, w_value], f32_rows,
        [narrow, narrow, square, narrow, square], narrow,
        deps=step(first) + step(last) + step(late) + [whole_up],
    )
    last = gather_pair(order, finish(last))
    first, last, late = [finish(part) for part in (first, last, late)]
    first, last = [[chunk.reshape(width, width) for chunk in pair] for pair in
                   [pair if len(pair) == 2 else [pair[0][0], pair[0][1]] for pair in (first, last)]]

    bits = down.ndim - 3
    whole_down = jnp.moveaxis(down, bits, 1).reshape(ff, width)
    return (
        result[None], input_grad[None],
        first[1], last[0], last[1], first[0],
        whole_up, whole_down,
        small[6], late[0], late[1], small[5], small[7:].reshape(ff), small[2],
        small[3], small[4], small[0], small[1],
    )


def solution(mesh):
    tokens = P("row", "seq", None)
    bucket = P("row", None)
    return jax.shard_map(
        on_device,
        mesh=mesh,
        in_specs=(tokens,) + (P(),) * 17 + (bucket, bucket, tokens),
        out_specs=(tokens, tokens) + (P(),) * 16,
        check_vma=False,
    )
```
